32 devices in a mesh: parts: 2 (over x), blk: 8 (over z, y), pair: 2 (over core).
Axes of the slice: x: 2, y: 2, z: 4, core: 2. Of those that a mesh axis runs over, the one named last changes fastest.
Arguments:
- queries: bfloat16 [28672, 768], P(('parts', 'blk', 'pair')), parts along dimension 0, may hold values from -50 to 50, as said below
- key_rows: bfloat16 [2048, 768], P(('parts', 'blk', 'pair')), parts along dimension 0, may hold values from -12 to 12, as said below
- label_rows: bfloat16 [2048, 1000], P(('parts', 'blk', 'pair')), parts along dimension 0, may hold values from -16 to 16
Outputs:
- corrected: bfloat16 [28672, 1000], P(('parts', 'blk', 'pair')), parts along dimension 0
The draws below stay inside these ranges and needn't reach their ends.
There are 2 independent parts, one for each index of `parts`. The reference program is written for one: setup_inputs(seed, part) draws one part's arguments, and reference() takes and returns one part's arrays. A program takes and returns all parts, laid end to end along the dimension named above; each array names one. Nothing has to cross between parts.
Inputs may be any that keep to these rules, and one draw needn't show every extreme that they name: `queries`: query embeddings; rows have different scales. `key_rows`: corpus embeddings; rows have different scales.
All inputs are finite; a program needn't handle non-finite values.
Results may differ from the reference program's by a relative error of at most 0.0045.
Values may be sent and summed in bfloat16 or wider, within the bound.
No kernel may reach another device: no remote copies, remote signals or barrier semaphores. Data moves between devices by JAX's collectives and lax.ppermute only.
A program may use at most 128 MiB of HBM per device.

```python
import math
import jax
import jax.numpy as jnp
import numpy as np
from jax import lax

E = 768
C = 1000
NQ = 14336
NK = 1024


def key_field(key, low_scale, high_scale):
    base = jnp.clip(jax.random.normal(jax.random.fold_in(key, 11), (NK, E), jnp.float32), -4.0, 4.0)
    scales = jnp.exp(jax.random.uniform(jax.random.fold_in(key, 12), (NK, 1), jnp.float32, np.log(low_scale), np.log(high_scale)))
    field = base * scales
    anchors = np.arange(8) * NK // 8
    field = field.at[anchors].set(base[anchors])
    field = field.at[anchors + 1].set(0.99 * base[anchors] + 0.1 * base[anchors + 1])
    return field


def draw_key_rows(key, part):
    field = key_field(key, 0.6, 1.6)
    return field.astype(jnp.bfloat16)


def draw_queries(key, part):
    own_key = jax.random.fold_in(key, 7)
    values = jnp.clip(jax.random.normal(jax.random.fold_in(own_key, 1), (NQ, E), jnp.float32), -4.0, 4.0)
    scales = jnp.exp(jax.random.uniform(jax.random.fold_in(own_key, 2), (NQ, 1), jnp.float32, np.log(0.5), np.log(2.5)))
    field = values * scales
    return field.astype(jnp.bfloat16)


def block_scale(rng, dims, split, low, top_value):
    loudness, own = 1.0, jax.random.fold_in(rng, 6)
    for position, shards_of in split:
        heights = jnp.exp(jax.random.uniform(jax.random.fold_in(own, position), (shards_of,), jnp.float32, low / len(split), top_value / len(split)))
        loudness = loudness * jnp.repeat(heights, dims[position] // shards_of).reshape([-1 if axis == position else 1 for axis in range(len(dims))])
    return loudness


def normal_values(key, shape, width, bound, cuts=(), dtype=jnp.bfloat16):
    values = jax.random.normal(key, shape, jnp.float32) * width
    if len(cuts) > 0:
        values = block_scale(key, shape, cuts, -0.22, 0.18) * values
    return jnp.clip(values, min=-bound, max=bound).astype(dtype)


def setup_inputs(seed: int = 0, part: int = 0) -> dict:
    key_of = jax.random.split(jax.random.key(seed), 4)
    own_keys = jax.random.split(jax.random.fold_in(key_of[3], part), 4)
    queries = draw_queries(jax.random.fold_in(jax.random.fold_in(key_of[3], part), 71), part)
    key_rows = draw_key_rows(jax.random.fold_in(jax.random.fold_in(key_of[3], part), 71), part)
    label_rows = normal_values(own_keys[2], (NK, C), 4.0, 16.0, ((0, 16),))
    return dict(queries=queries, key_rows=key_rows, label_rows=label_rows)


def reference(queries, key_rows, label_rows):
    query_count = queries.shape[0]
    block_rows = math.gcd(query_count, 2048)
    score_scale = E ** -0.5

    def one_block(query_block):
        scores = jnp.dot(query_block, key_rows.T, preferred_element_type=jnp.float32) * score_scale
        row_max = jnp.max(scores, axis=1, keepdims=True)
        weights = jnp.exp(scores - row_max)
        totals = jnp.sum(weights, axis=1)
        weighted = jnp.dot(weights.astype(jnp.bfloat16), label_rows, preferred_element_type=jnp.float32)
        return (weighted / totals[:, None]).astype(jnp.bfloat16)

    stacked = queries.reshape(query_count // block_rows, block_rows, queries.shape[1])
    result = lax.map(one_block, stacked)
    return result.reshape(query_count, label_rows.shape[1])
```

```python
import jax
import jax.numpy as jnp
from jax import lax
from jax.experimental import pallas as pl
from jax.experimental.pallas import tpu as pltpu
from jax.sharding import PartitionSpec as P

AXES = ("blk", "pair")


def ring_of(chips):
    if chips == 8:
        return [0, 2, 4, 6, 7, 5, 3, 1]
    return list(range(chips))


def hop(ring, shift, swap):
    n, out = len(ring), []
    for place, chip in enumerate(ring):
        for core in range(2):
            step = shift if core == 0 else -shift
            out.append((chip * 2 + core, ring[(place + step) % n] * 2 + (core ^ swap)))
    return out


def attend(width, scale, count, *refs):
    q_ref, pieces, out_ref = refs[0], refs[1 : 1 + count], refs[1 + count]
    keys = jnp.concatenate([p[:, :width] for p in pieces], axis=0)
    labels = jnp.concatenate([p[:, width:] for p in pieces], axis=0)
    rows = q_ref.shape[0]
    for low in range(0, rows, 128):
        high = min(low + 128, rows)
        scores = (
            lax.dot_general(
                keys, q_ref[low:high, :], (((1,), (1,)), ((), ())), preferred_element_type=jnp.float32
            )
            * scale
        )
        weights = jnp.exp(scores - jnp.max(scores, axis=0, keepdims=True))
        totals = jnp.sum(weights, axis=0, keepdims=True)
        weighted = lax.dot_general(
            labels, weights.astype(jnp.bfloat16), (((0,), (0,)), ((), ())), preferred_element_type=jnp.float32
        )
        out_ref[:, low:high] = (weighted / totals).astype(jnp.bfloat16)


def on_device(queries, key_rows, label_rows, chips):
    width, classes = key_rows.shape[1], label_rows.shape[1]
    half = key_rows.shape[0]
    ring = ring_of(chips)
    same, cross, swap = hop(ring, 1, 0), hop(ring, -1, 1), hop(ring, 0, 1)

    def send(x, pairs):
        return lax.ppermute(x, AXES, pairs)

    def beside(k, l):
        return jnp.concatenate([k, l], axis=1)

    pieces = [beside(key_rows, label_rows), beside(send(key_rows, swap), send(label_rows, swap))]
    first = beside(send(key_rows, same), send(label_rows, same))
    second = beside(send(key_rows, cross), send(label_rows, cross))
    for step in range(1, chips // 2 + 1):
        last = step == chips // 2
        here = [first] if last else [first, second]
        pieces += here + [send(x, swap) for x in here]
        if not last:
            first = send(first, same)
            if step + 1 < chips // 2:
                second = send(second, same)
    rows = queries.shape[0]
    out = pl.pallas_call(
        lambda *refs: attend(width, width**-0.5, len(pieces), *refs),
        out_shape=jax.ShapeDtypeStruct((classes, rows), jnp.bfloat16),
        in_specs=[pl.BlockSpec(memory_space=pltpu.VMEM)] * (1 + len(pieces)),
        out_specs=pl.BlockSpec(memory_space=pltpu.VMEM),
        compiler_params=pltpu.CompilerParams(vmem_limit_bytes=56 * 2**20),
    )(queries, *pieces)
    return out.T


def solution(mesh):
    chips = mesh.shape["blk"]
    spec = P(("parts", "blk", "pair"), None)
    return jax.shard_map(
        lambda q, k, l: on_device(q, k, l, chips),
        mesh=mesh,
        in_specs=(spec, spec, spec),
        out_specs=spec,
        check_vma=False,
    )
```

```python
import functools

import jax
import jax.numpy as jnp
from jax import lax
from jax.experimental import pallas as pl
from jax.experimental.pallas import tpu as pltpu
from jax.sharding import PartitionSpec as P

AXES = ("blk", "pair")
F32, BF16 = jnp.float32, jnp.bfloat16
WHOLE = pl.BlockSpec(memory_space=pltpu.VMEM)
PARAMS = pltpu.CompilerParams(vmem_limit_bytes=28 * 2**20)


def ring_of(chips):
    if chips == 8:
        return [0, 2, 4, 6, 7, 5, 3, 1]
    return list(range(chips))


def hop(ring, shift):
    n, out = len(ring), []
    for place, chip in enumerate(ring):
        for core, step in ((0, shift), (1, -shift)):
            out.append((chip * 2 + core, ring[(place + step) % n] * 2 + 1 - core))
    return out


def begin(q_hbm, k_hbm, l_hbm, top_ref, totals_ref, weighted_ref, q_ref, own_ref, q_in, k_in, l_in, sem):
    copies = [
        pltpu.make_async_copy(source, target, sem.at[n])
        for n, (source, target) in enumerate([(k_hbm, k_in), (l_hbm, l_in), (q_hbm, q_in)])
    ]
    for copy in copies:
        copy.start()
    for copy in copies:
        copy.wait()
    keys, labels, q = k_in[...], l_in[...], q_in[...].T
    width = keys.shape[1]
    own_ref[:, :width] = keys
    own_ref[:, width:] = labels
    q_ref[...] = q
    scores = jnp.dot(keys, q, preferred_element_type=F32) * width**-0.5
    top = jnp.max(scores, axis=0, keepdims=True)
    weights = jnp.exp(scores - top)
    top_ref[...] = top
    totals_ref[...] = jnp.sum(weights, axis=0, keepdims=True)
    weighted_ref[...] = jnp.dot(labels.T, weights.astype(BF16), preferred_element_type=F32)


def begin_call(queries, key_rows, label_rows):
    (rows, width), (count, classes) = queries.shape, label_rows.shape
    row = jax.ShapeDtypeStruct((1, rows), F32)
    operands = [pltpu.with_memory_space_constraint(x, pltpu.HBM) for x in (queries, key_rows, label_rows)]
    return pl.pallas_call(
        begin,
        out_shape=[
            row,
            row,
            jax.ShapeDtypeStruct((classes, rows), F32),
            jax.ShapeDtypeStruct((width, rows), BF16),
            jax.ShapeDtypeStruct((count, width + classes), BF16),
        ],
        in_specs=[pl.BlockSpec(memory_space=pltpu.HBM)] * 3,
        out_specs=[WHOLE] * 5,
        scratch_shapes=[
            pltpu.VMEM((rows, width), BF16),
            pltpu.VMEM((count, width), BF16),
            pltpu.VMEM((count, classes), BF16),
            pltpu.SemaphoreType.DMA((3,)),
        ],
        compiler_params=PARAMS,
    )(*operands)


def absorb(width, count, last, *refs):
    q_ref, pieces, (old_top, old_totals, old_weighted) = refs[0], refs[1 : 1 + count], refs[1 + count : 4 + count]
    refs = refs[4 + count :]
    keys = jnp.concatenate([p[:, :width] for p in pieces], axis=0)
    labels = jnp.concatenate([p[:, width:] for p in pieces], axis=0).T
    scores = jnp.dot(keys, q_ref[...], preferred_element_type=F32) * width**-0.5
    top = jnp.maximum(old_top[...], jnp.max(scores, axis=0, keepdims=True))
    factor = jnp.exp(old_top[...] - top)
    weights = jnp.exp(scores - top)
    totals = jnp.sum(weights, axis=0, keepdims=True) + old_totals[...] * factor
    weights = weights.astype(BF16)
    if not last:
        refs[0][...], refs[1][...] = top, totals
        refs[2][...] = jnp.dot(labels, weights, preferred_element_type=F32) + old_weighted[...] * factor
        return
    out_ref, done_ref, sem = refs
    rows, copies = weights.shape[1], []
    middle = rows // 256 * 128
    for n, (low, high) in enumerate([(0, middle), (middle, rows)]):
        weighted = jnp.dot(labels, weights[:, low:high], preferred_element_type=F32)
        weighted += old_weighted[:, low:high] * factor[:, low:high]
        done_ref[:, low:high] = (weighted / totals[:, low:high]).astype(BF16)
        copies.append(pltpu.make_async_copy(done_ref.at[:, low:high], out_ref.at[:, low:high], sem.at[n]))
        copies[-1].start()
    for copy in copies:
        copy.wait()


def absorb_call(q, pieces, state, last):
    (width, rows), classes = q.shape, state[2].shape[0]
    if last:
        shapes = [jax.ShapeDtypeStruct((classes, rows), BF16)]
        places = [pl.BlockSpec(memory_space=pl.ANY)]
        scratch = [pltpu.VMEM((classes, rows), BF16), pltpu.SemaphoreType.DMA((2,))]
    else:
        shapes, places, scratch = [jax.ShapeDtypeStruct(s.shape, F32) for s in state], [WHOLE] * 3, []
    operands = (q, *pieces, *state)
    return pl.pallas_call(
        functools.partial(absorb, width, len(pieces), last),
        out_shape=shapes,
        in_specs=[WHOLE] * len(operands),
        out_specs=places,
        scratch_shapes=scratch,
        compiler_params=PARAMS,
    )(*operands)


def on_device(queries, key_rows, label_rows, chips):
    half, ring = chips // 2, ring_of(chips)
    ways = hop(ring, -1), hop(ring, 1)
    cores = [(2 * chip + core, 2 * chip + 1 - core) for chip in ring for core in range(2)]

    def send(x, pairs):
        return lax.ppermute(x, AXES, pairs)

    x = jnp.concatenate([send(key_rows, ways[0]), send(label_rows, ways[0])], axis=1)
    *state, q, own = begin_call(queries, key_rows, label_rows)
    y = send(own, ways[1])
    pieces = {1: [send(own, cores)]}
    absorbed = 0

    def absorb_to(step):
        nonlocal state, absorbed
        while absorbed < step:
            absorbed += 1
            state = absorb_call(q, pieces[absorbed], state, absorbed == half)

    for step in range(1, half + 1):
        pieces.setdefault(step, [])
        if step < half:
            x_next = send(x, ways[step % 2])
        else:
            absorb_to(half - 2)
            x, state = lax.optimization_barrier((x, state))
        pieces[step] += [x, send(x, cores)]
        if step < half:
            pieces[step] += [y, send(y, cores)]
            if step < half - 1:
                y = send(y, ways[1 - step % 2])
            x = x_next
    absorb_to(half)
    return state[0].T


def solution(mesh):
    chips = mesh.shape["blk"]
    spec = P(("parts", "blk", "pair"), None)
    return jax.shard_map(
        lambda q, k, l: on_device(q, k, l, chips),
        mesh=mesh,
        in_specs=(spec, spec, spec),
        out_specs=spec,
        check_vma=False,
    )
```

```python
import functools

import jax
import jax.numpy as jnp
from jax import lax
from jax.experimental import pallas as pl
from jax.experimental.pallas import tpu as pltpu
from jax.sharding import PartitionSpec as P

AXES = ("blk", "pair")
F32, BF16 = jnp.float32, jnp.bfloat16
WHOLE = pl.BlockSpec(memory_space=pltpu.VMEM)
PARAMS = pltpu.CompilerParams(vmem_limit_bytes=28 * 2**20)


def ring_of(chips):
    if chips == 8:
        return [0, 2, 4, 6, 7, 5, 3, 1]
    return list(range(chips))


def hop(ring, shift):
    n, out = len(ring), []
    for place, chip in enumerate(ring):
        for core, step in ((0, shift), (1, -shift)):
            out.append((chip * 2 + core, ring[(place + step) % n] * 2 + 1 - core))
    return out


def begin(q_hbm, k_hbm, l_hbm, q_ref, own_ref, q_in, k_in, l_in, sem):
    copies = [
        pltpu.make_async_copy(source, target, sem.at[n])
        for n, (source, target) in enumerate([(k_hbm, k_in), (l_hbm, l_in), (q_hbm, q_in)])
    ]
    for copy in copies:
        copy.start()
    for copy in copies:
        copy.wait()
    width = k_in.shape[1]
    own_ref[:, :width] = k_in[...]
    own_ref[:, width:] = l_in[...]
    q_ref[...] = q_in[...].T


def begin_call(queries, key_rows, label_rows):
    (rows, width), (count, classes) = queries.shape, label_rows.shape
    operands = [pltpu.with_memory_space_constraint(x, pltpu.HBM) for x in (queries, key_rows, label_rows)]
    return pl.pallas_call(
        begin,
        out_shape=[
            jax.ShapeDtypeStruct((width, rows), BF16),
            jax.ShapeDtypeStruct((count, width + classes), BF16),
        ],
        in_specs=[pl.BlockSpec(memory_space=pltpu.HBM)] * 3,
        out_specs=[WHOLE] * 2,
        scratch_shapes=[
            pltpu.VMEM((rows, width), BF16),
            pltpu.VMEM((count, width), BF16),
            pltpu.VMEM((count, classes), BF16),
            pltpu.SemaphoreType.DMA((3,)),
        ],
        compiler_params=PARAMS,
    )(*operands)


def absorb(width, count, first, last, *refs):
    q_ref, pieces, refs = refs[0], refs[1 : 1 + count], refs[1 + count :]
    keys = jnp.concatenate([p[:, :width] for p in pieces], axis=0)
    labels = jnp.concatenate([p[:, width:] for p in pieces], axis=0).T
    scores = jnp.dot(keys, q_ref[...], preferred_element_type=F32) * width**-0.5
    top = jnp.max(scores, axis=0, keepdims=True)
    if not first:
        (old_top, old_totals, old_weighted), refs = refs[:3], refs[3:]
        top = jnp.maximum(old_top[...], top)
        factor = jnp.exp(old_top[...] - top)
    weights = jnp.exp(scores - top)
    totals = jnp.sum(weights, axis=0, keepdims=True)
    if not first:
        totals += old_totals[...] * factor
    weights = weights.astype(BF16)

    def weighted(low, high):
        new = jnp.dot(labels, weights[:, low:high], preferred_element_type=F32)
        return new if first else new + old_weighted[:, low:high] * factor[:, low:high]

    rows = weights.shape[1]
    if not last:
        refs[0][...], refs[1][...], refs[2][...] = top, totals, weighted(0, rows)
        return
    out_ref, done_ref, sem = refs
    copies, middle = [], rows // 256 * 128
    for n, (low, high) in enumerate([(0, middle), (middle, rows)]):
        done_ref[:, low:high] = (weighted(low, high) / totals[:, low:high]).astype(BF16)
        copies.append(pltpu.make_async_copy(done_ref.at[:, low:high], out_ref.at[:, low:high], sem.at[n]))
        copies[-1].start()
    for copy in copies:
        copy.wait()


def absorb_call(q, pieces, state, last):
    (width, rows), classes = q.shape, pieces[0].shape[1] - q.shape[0]
    if last:
        shapes = [jax.ShapeDtypeStruct((classes, rows), BF16)]
        places = [pl.BlockSpec(memory_space=pl.ANY)]
        scratch = [pltpu.VMEM((classes, rows), BF16), pltpu.SemaphoreType.DMA((2,))]
    else:
        shapes, places, scratch = [jax.ShapeDtypeStruct((n, rows), F32) for n in (1, 1, classes)], [WHOLE] * 3, []
    operands = (q, *pieces, *state)
    return pl.pallas_call(
        functools.partial(absorb, width, len(pieces), not state, last),
        out_shape=shapes,
        in_specs=[WHOLE] * len(operands),
        out_specs=places,
        scratch_shapes=scratch,
        compiler_params=PARAMS,
    )(*operands)


def on_device(queries, key_rows, label_rows, chips):
    half, ring = chips // 2, ring_of(chips)
    ways = hop(ring, -1), hop(ring, 1)
    cores = [(2 * chip + core, 2 * chip + 1 - core) for chip in ring for core in range(2)]

    def send(x, pairs):
        return lax.ppermute(x, AXES, pairs)

    x = jnp.concatenate([send(key_rows, ways[0]), send(label_rows, ways[0])], axis=1)
    q, own = begin_call(queries, key_rows, label_rows)
    y = send(own, ways[1])
    groups = [[own, send(own, cores), x]] + [[] for _ in range(half)]
    state, absorbed = (), 0

    def absorb_to(count):
        nonlocal state, absorbed
        while absorbed < count:
            state = absorb_call(q, groups[absorbed], state, absorbed == half)
            absorbed += 1

    def absorb_before(count, piece):
        nonlocal state
        absorb_to(count)
        piece, state = lax.optimization_barrier((piece, state))
        return piece

    for step in range(1, half + 1):
        if step < half:
            x_next = send(x, ways[step % 2])
            if step == 1:
                y = absorb_before(1, y)
            if step < half - 1:
                y_next = send(y, ways[1 - step % 2])
            groups[step] += [send(x, cores), y, send(y, cores)] + ([x] if step > 1 else [])
            x, y = x_next, y_next
        else:
            x = absorb_before(half - 1, x)
            groups[half] += [x, send(x, cores)]
    absorb_to(half + 1)
    return state[0].T


def solution(mesh):
    chips = mesh.shape["blk"]
    spec = P(("parts", "blk", "pair"), None)
    return jax.shard_map(
        lambda q, k, l: on_device(q, k, l, chips),
        mesh=mesh,
        in_specs=(spec, spec, spec),
        out_specs=spec,
        check_vma=False,
    )
```

```python
import functools

import jax
import jax.numpy as jnp
from jax import lax
from jax.experimental import pallas as pl
from jax.experimental.pallas import tpu as pltpu
from jax.sharding import PartitionSpec as P

AXES = ("blk", "pair")
F32, BF16 = jnp.float32, jnp.bfloat16
WHOLE = pl.BlockSpec(memory_space=pltpu.VMEM)
PARAMS = pltpu.CompilerParams(vmem_limit_bytes=28 * 2**20)


def ring_of(chips):
    if chips == 8:
        return [0, 2, 4, 6, 7, 5, 3, 1]
    return list(range(chips))


def hop(ring, shift):
    n, out = len(ring), []
    for place, chip in enumerate(ring):
        for core, step in ((0, shift), (1, -shift)):
            out.append((chip * 2 + core, ring[(place + step) % n] * 2 + 1 - core))
    return out


def begin(q_hbm, k_hbm, l_hbm, q_ref, own_ref, q_in, k_in, l_in, sem):
    rows, width = q_in.shape
    middle = rows // 256 * 128
    spans = [(0, middle), (middle, rows)]
    parts = [(k_hbm, k_in), (l_hbm, l_in)] + [(q_hbm.at[low:high], q_in.at[low:high]) for low, high in spans]
    copies = [pltpu.make_async_copy(source, target, sem.at[n]) for n, (source, target) in enumerate(parts)]
    for copy in copies:
        copy.start()
    copies[0].wait()
    own_ref[:, :width] = k_in[...]
    copies[1].wait()
    own_ref[:, width:] = l_in[...]
    for copy, (low, high) in zip(copies[2:], spans):
        copy.wait()
        q_ref[:, low:high] = q_in[low:high, :].T


def begin_call(queries, key_rows, label_rows):
    (rows, width), (count, classes) = queries.shape, label_rows.shape
    operands = [pltpu.with_memory_space_constraint(x, pltpu.HBM) for x in (queries, key_rows, label_rows)]
    return pl.pallas_call(
        begin,
        out_shape=[
            jax.ShapeDtypeStruct((width, rows), BF16),
            jax.ShapeDtypeStruct((count, width + classes), BF16),
        ],
        in_specs=[pl.BlockSpec(memory_space=pltpu.HBM)] * 3,
        out_specs=[WHOLE] * 2,
        scratch_shapes=[
            pltpu.VMEM((rows, width), BF16),
            pltpu.VMEM((count, width), BF16),
            pltpu.VMEM((count, classes), BF16),
            pltpu.SemaphoreType.DMA((4,)),
        ],
        compiler_params=PARAMS,
    )(*operands)


def absorb(width, count, first, last, *refs):
    q_ref, pieces, refs = refs[0], refs[1 : 1 + count], refs[1 + count :]
    keys = jnp.concatenate([p[:, :width] for p in pieces], axis=0)
    labels = jnp.concatenate([p[:, width:] for p in pieces], axis=0).T
    scores = jnp.dot(keys, q_ref[...], preferred_element_type=F32) * width**-0.5
    top = jnp.max(scores, axis=0, keepdims=True)
    if not first:
        (old_top, old_totals, old_weighted), refs = refs[:3], refs[3:]
        top = jnp.maximum(old_top[...], top)
        factor = jnp.exp(old_top[...] - top)
    weights = jnp.exp(scores - top)
    totals = jnp.sum(weights, axis=0, keepdims=True)
    if not first:
        totals += old_totals[...] * factor
    weights = weights.astype(BF16)

    def weighted(low, high):
        new = jnp.dot(labels, weights[:, low:high], preferred_element_type=F32)
        return new if first else new + old_weighted[:, low:high] * factor[:, low:high]

    rows = weights.shape[1]
    if not last:
        refs[0][...], refs[1][...], refs[2][...] = top, totals, weighted(0, rows)
        return
    out_ref, done_ref, sem = refs
    copies, middle = [], rows // 256 * 128
    for n, (low, high) in enumerate([(0, middle), (middle, rows)]):
        done_ref[:, low:high] = (weighted(low, high) / totals[:, low:high]).astype(BF16)
        copies.append(pltpu.make_async_copy(done_ref.at[:, low:high], out_ref.at[:, low:high], sem.at[n]))
        copies[-1].start()
    for copy in copies:
        copy.wait()


def absorb_call(q, pieces, state, last):
    (width, rows), classes = q.shape, pieces[0].shape[1] - q.shape[0]
    if last:
        shapes = [jax.ShapeDtypeStruct((classes, rows), BF16)]
        places = [pl.BlockSpec(memory_space=pl.ANY)]
        scratch = [pltpu.VMEM((classes, rows), BF16), pltpu.SemaphoreType.DMA((2,))]
    else:
        shapes, places, scratch = [jax.ShapeDtypeStruct((n, rows), F32) for n in (1, 1, classes)], [WHOLE] * 3, []
    operands = (q, *pieces, *state)
    return pl.pallas_call(
        functools.partial(absorb, width, len(pieces), not state, last),
        out_shape=shapes,
        in_specs=[WHOLE] * len(operands),
        out_specs=places,
        scratch_shapes=scratch,
        compiler_params=PARAMS,
    )(*operands)


def on_device(queries, key_rows, label_rows, chips):
    half, ring = chips // 2, ring_of(chips)
    ways = hop(ring, -1), hop(ring, 1)
    cores = [(2 * chip + core, 2 * chip + 1 - core) for chip in ring for core in range(2)]

    def send(x, pairs):
        return lax.ppermute(x, AXES, pairs)

    x = jnp.concatenate([send(key_rows, ways[0]), send(label_rows, ways[0])], axis=1)
    q, own = begin_call(queries, key_rows, label_rows)
    y = send(own, ways[1])
    groups = [[own, send(own, cores), x]] + [[] for _ in range(half)]
    state, absorbed = (), 0

    def absorb_to(count):
        nonlocal state, absorbed
        while absorbed < count:
            state = absorb_call(q, groups[absorbed], state, absorbed == half)
            absorbed += 1

    def absorb_before(count, piece):
        nonlocal state
        absorb_to(count)
        piece, state = lax.optimization_barrier((piece, state))
        return piece

    for step in range(1, half + 1):
        if step < half:
            x_next = send(x, ways[step % 2])
            if step == 1:
                y = absorb_before(1, y)
            if step < half - 1:
                y_next = send(y, ways[1 - step % 2])
            groups[step] += [send(x, cores), y, send(y, cores)] + ([x] if step > 1 else [])
            x, y = x_next, y_next
        else:
            x = absorb_before(half - 1, x)
            groups[half] += [x, send(x, cores)]
    absorb_to(half + 1)
    return state[0].T


def solution(mesh):
    chips = mesh.shape["blk"]
    spec = P(("parts", "blk", "pair"), None)
    return jax.shard_map(
        lambda q, k, l: on_device(q, k, l, chips),
        mesh=mesh,
        in_specs=(spec, spec, spec),
        out_specs=spec,
        check_vma=False,
    )
```

```python
import functools

import jax
import jax.numpy as jnp
from jax import lax
from jax.experimental import pallas as pl
from jax.experimental.pallas import tpu as pltpu
from jax.sharding import PartitionSpec as P

AXES = ("blk", "pair")
F32, BF16 = jnp.float32, jnp.bfloat16
WHOLE = pl.BlockSpec(memory_space=pltpu.VMEM)
PARAMS = pltpu.CompilerParams(vmem_limit_bytes=28 * 2**20)


def ring_of(chips):
    if chips == 8:
        return [0, 2, 4, 6, 7, 5, 3, 1]
    return list(range(chips))


def hop(ring, shift):
    n, out = len(ring), []
    for place, chip in enumerate(ring):
        for core, step in ((0, shift), (1, -shift)):
            out.append((chip * 2 + core, ring[(place + step) % n] * 2 + 1 - core))
    return out


def begin(q_hbm, k_hbm, l_hbm, q_ref, own_ref, q_in, k_in, l_in, sem):
    rows, width = q_in.shape
    middle = rows // 256 * 128
    spans = [(0, middle), (middle, rows)]
    parts = [(k_hbm, k_in), (l_hbm, l_in)] + [(q_hbm.at[low:high], q_in.at[low:high]) for low, high in spans]
    copies = [pltpu.make_async_copy(source, target, sem.at[n]) for n, (source, target) in enumerate(parts)]
    for copy in copies:
        copy.start()
    copies[0].wait()
    own_ref[:, :width] = k_in[...]
    copies[1].wait()
    own_ref[:, width:] = l_in[...]
    for copy, (low, high) in zip(copies[2:], spans):
        copy.wait()
        q_ref[:, low:high] = q_in[low:high, :].T


def begin_call(queries, key_rows, label_rows):
    (rows, width), (count, classes) = queries.shape, label_rows.shape
    operands = [pltpu.with_memory_space_constraint(x, pltpu.HBM) for x in (queries, key_rows, label_rows)]
    return pl.pallas_call(
        begin,
        out_shape=[
            jax.ShapeDtypeStruct((width, rows), BF16),
            jax.ShapeDtypeStruct((count, width + classes), BF16),
        ],
        in_specs=[pl.BlockSpec(memory_space=pltpu.HBM)] * 3,
        out_specs=[WHOLE] * 2,
        scratch_shapes=[
            pltpu.VMEM((rows, width), BF16),
            pltpu.VMEM((count, width), BF16),
            pltpu.VMEM((count, classes), BF16),
            pltpu.SemaphoreType.DMA((4,)),
        ],
        compiler_params=PARAMS,
    )(*operands)


def absorb(width, count, first, last, *refs):
    q_ref, pieces, refs = refs[0], refs[1 : 1 + count], refs[1 + count :]
    keys = jnp.concatenate([p[:, :width] for p in pieces], axis=0)
    labels = jnp.concatenate([p[:, width:] for p in pieces], axis=0).T
    scores = jnp.dot(keys, q_ref[...], preferred_element_type=F32) * width**-0.5
    top = jnp.max(scores, axis=0, keepdims=True)
    if not first:
        (old_top, old_totals, old_weighted), refs = refs[:3], refs[3:]
        top = jnp.maximum(old_top[...], top)
        factor = jnp.exp(old_top[...] - top)
    weights = jnp.exp(scores - top)
    totals = jnp.sum(weights, axis=0, keepdims=True)
    if not first:
        totals += old_totals[...] * factor
    weights = weights.astype(BF16)

    def weighted(low, high):
        new = jnp.dot(labels, weights[:, low:high], preferred_element_type=F32)
        return new if first else new + old_weighted[:, low:high] * factor[:, low:high]

    rows = weights.shape[1]
    if not last:
        refs[0][...], refs[1][...], refs[2][...] = top, totals, weighted(0, rows)
        return
    out_ref, done_ref, sem = refs
    copies, middle = [], rows // 256 * 128
    for n, (low, high) in enumerate([(0, middle), (middle, rows)]):
        done_ref[:, low:high] = (weighted(low, high) / totals[:, low:high]).astype(BF16)
        copies.append(pltpu.make_async_copy(done_ref.at[:, low:high], out_ref.at[:, low:high], sem.at[n]))
        copies[-1].start()
    for copy in copies:
        copy.wait()


def absorb_call(q, pieces, state, last):
    (width, rows), classes = q.shape, pieces[0].shape[1] - q.shape[0]
    if last:
        shapes = [jax.ShapeDtypeStruct((classes, rows), BF16)]
        places = [pl.BlockSpec(memory_space=pl.ANY)]
        scratch = [pltpu.VMEM((classes, rows), BF16), pltpu.SemaphoreType.DMA((2,))]
    else:
        shapes, places, scratch = [jax.ShapeDtypeStruct((n, rows), F32) for n in (1, 1, classes)], [WHOLE] * 3, []
    operands = (q, *pieces, *state)
    return pl.pallas_call(
        functools.partial(absorb, width, len(pieces), not state, last),
        out_shape=shapes,
        in_specs=[WHOLE] * len(operands),
        out_specs=places,
        scratch_shapes=scratch,
        compiler_params=PARAMS,
    )(*operands)


def on_device(queries, key_rows, label_rows, chips):
    half, ring = chips // 2, ring_of(chips)
    ways = hop(ring, -1), hop(ring, 1)
    cores = [(2 * chip + core, 2 * chip + 1 - core) for chip in ring for core in range(2)]

    def send(x, pairs):
        return lax.ppermute(x, AXES, pairs)

    x = jnp.concatenate([send(key_rows, ways[0]), send(label_rows, ways[0])], axis=1)
    q, own = begin_call(queries, key_rows, label_rows)
    y = send(own, ways[1])
    groups = [[own, send(own, cores), x]] + [[] for _ in range(half)]
    state, absorbed = (), 0

    def absorb_to(count):
        nonlocal state, absorbed
        while absorbed < count:
            state = absorb_call(q, groups[absorbed], state, absorbed == half)
            absorbed += 1

    def absorb_before(count, piece):
        nonlocal state
        absorb_to(count)
        piece, state = lax.optimization_barrier((piece, state))
        return piece

    for step in range(1, half + 1):
        if step < half:
            x_next = send(x, ways[step % 2])
            if step == 1:
                y = absorb_before(1, y)
            if step == half - 1:
                y = absorb_before(half - 2, y)
            if step < half - 1:
                y_next = send(y, ways[1 - step % 2])
            both = jnp.concatenate([x, y], axis=0)
            groups[step] += [send(both, cores), y] + ([x] if step > 1 else [])
            x, y = x_next, y_next
        else:
            x = absorb_before(half - 1, x)
            groups[half] += [x, send(x, cores)]
    absorb_to(half + 1)
    return state[0].T


def solution(mesh):
    chips = mesh.shape["blk"]
    spec = P(("parts", "blk", "pair"), None)
    return jax.shard_map(
        lambda q, k, l: on_device(q, k, l, chips),
        mesh=mesh,
        in_specs=(spec, spec, spec),
        out_specs=spec,
        check_vma=False,
    )
```
